32 devices in a mesh: gy: 4 (over y, x), gx: 8 (over z, core).
Axes of the slice: x: 2, y: 2, z: 4, core: 2. Of those that a mesh axis runs over, the one named last changes fastest.
Arguments:
- fields: bfloat16 [4, 16, 16384], P('gy', None, 'gx'), may hold values from -6 to 6
- leaf_inverse: bfloat16 [4, 64, 256, 256], P('gy', 'gx'), may hold values from -0.375 to 0.375
- coupling: bfloat16 [4, 64, 64, 256], P('gy', 'gx'), may hold values from -0.375 to 0.375
- skeleton_index: int32 [4, 64, 64], P('gy', 'gx'), may hold values from 0 to 255, as said below
- up_coef: float32 [4, 24, 4, 512], P('gy', 'gx'), may hold values from -0.5 to 0.5
- down_coef: float32 [4, 24, 4, 512], P('gy', 'gx'), may hold values from -0.5 to 0.5
- merge_own: bfloat16 [4, 24, 512, 512], P('gy', 'gx'), may hold values from -0.1875 to 0.1875
- merge_other: bfloat16 [4, 24, 512, 512], P('gy', 'gx'), may hold values from -0.1875 to 0.1875
- top_inverse: bfloat16 [4, 4096, 512], P('gy', 'gx'), may hold values from -0.1875 to 0.1875
- compress: bfloat16 [4, 256, 512], P('gy', 'gx'), may hold values from -0.25 to 0.25
- top_couple: bfloat16 [1024, 1024], P(None, ('gy', 'gx')), may hold values from -0.375 to 0.375
Outputs:
- solution: float32 [4, 16, 16384], P('gy', None, 'gx')
The draws below stay inside these ranges and needn't reach their ends.
Inputs may be any that keep to these rules, and one draw needn't show every extreme that they name: `skeleton_index`: the 64 positions of one box are distinct.
All inputs are finite; a program needn't handle non-finite values.
Results may differ from the reference program's by a relative error of at most 0.015.
Values may be sent and summed in bfloat16 or wider, within the bound.
A program may use at most 64 MiB of HBM per device.

```python
import jax
import jax.numpy as jnp
import numpy as np
from jax import lax

F = 16
Q = 256
K = 64
NBX = 8
KT = 32
LEVELS = 3
M = 512
NPTS = 2048
N_GY = 4
N_GX = 8
DEVICES = 32


def draw_skeleton_index(key, part):
    count = N_GY * N_GX * NBX
    keys = jax.random.split(key, count)
    chosen = jax.vmap(lambda single: jax.random.permutation(single, Q)[:K])(keys)
    return chosen.reshape(N_GY, N_GX * NBX, K).astype(jnp.int32)


def strengthened(values, key, source, target, blocks, factor):
    owner, partner = [(jnp.arange(values.shape[position]) // (values.shape[position] // blocks)).reshape([-1 if axis == position else 1 for axis in range(values.ndim)]) for position in (source, target)]
    chosen = jax.random.permutation(key, blocks)[partner]
    strong = (owner == chosen) | (owner == (partner + blocks // 2) % blocks)
    return jnp.where(strong, factor * values, values)


def block_levels(stream_key, extent, pieces, least, largest):
    def one(dim, blocks):
        heights = jax.random.uniform(jax.random.fold_in(jax.random.fold_in(stream_key, 6), dim), (blocks,), jnp.float32, least / len(pieces), largest / len(pieces))
        return jnp.repeat(jnp.exp(heights), extent[dim] // blocks).reshape((-1,) + (1,) * (len(extent) - dim - 1))

    factor_of = one(*pieces[0])
    for cut in pieces[1:]:
        factor_of = factor_of * one(*cut)
    return factor_of


def centred(stream_key, extent, deviation, bound, pieces=(), held_as=jnp.bfloat16):
    array = jax.random.normal(stream_key, extent, jnp.float32) * deviation
    if len(pieces) > 0:
        array = block_levels(stream_key, extent, pieces, -0.22, 0.18) * array
    return jnp.clip(array, min=-bound, max=bound).astype(held_as)


def heavy_noise(key, shape, width, most, cuts, heavy, held_as=jnp.bfloat16):
    entries = width * jax.random.normal(key, shape, jnp.float32)
    if cuts:
        entries = entries * block_levels(key, shape, cuts, -0.22, 0.18)
    return jnp.clip(strengthened(entries, jax.random.fold_in(key, 3), *heavy), -most, most).astype(held_as)


def setup_inputs(seed: int = 0) -> dict:
    arg_keys = jax.random.split(jax.random.key(seed), 12)
    return {
        "fields": centred(arg_keys[0], (N_GY, F, N_GX * NPTS), 1.0, 6.0, ((0, 4), (2, 8))),
        "leaf_inverse": centred(arg_keys[1], (N_GY, N_GX * NBX, Q, Q), Q ** -0.5, 0.375, ((0, 4), (1, 8))),
        "coupling": centred(arg_keys[2], (N_GY, N_GX * NBX, K, Q), Q ** -0.5, 0.375, ((0, 4), (1, 8))),
        "skeleton_index": draw_skeleton_index(jax.random.fold_in(arg_keys[11], 71), 0),
        "up_coef": jnp.clip(jax.random.uniform(arg_keys[4], (N_GY, N_GX * LEVELS, 4, M), jnp.float32, -0.5, 0.5) * block_levels(arg_keys[4], (N_GY, N_GX * LEVELS, 4, M), ((0, 4), (1, 8)), -0.4, 0.0), -0.5, 0.5),
        "down_coef": jnp.clip(jax.random.uniform(arg_keys[5], (N_GY, N_GX * LEVELS, 4, M), jnp.float32, -0.5, 0.5) * block_levels(arg_keys[5], (N_GY, N_GX * LEVELS, 4, M), ((0, 4), (1, 8)), -0.4, 0.0), -0.5, 0.5),
        "merge_own": centred(arg_keys[6], (N_GY, N_GX * LEVELS, M, M), (2 * M) ** -0.5, 0.1875, ((0, 4), (1, 8))),
        "merge_other": centred(arg_keys[7], (N_GY, N_GX * LEVELS, M, M), (2 * M) ** -0.5, 0.1875, ((0, 4), (1, 8))),
        "top_inverse": centred(arg_keys[8], (N_GY, N_GX * M, M), (2 * M) ** -0.5, 0.1875, ((0, 4), (1, 8))),
        "compress": centred(arg_keys[9], (N_GY, N_GX * KT, M), M ** -0.5, 0.25, ((0, 4), (1, 8))),
        "top_couple": heavy_noise(arg_keys[10], (DEVICES * KT, DEVICES * KT), (DEVICES * KT) ** -0.5, 0.375, ((1, 32),), (0, 1, 32, 2.75)),
    }


def neighbour_mix(state, coefs):
    padded = jnp.pad(state, ((1, 1), (1, 1), (0, 0), (0, 0)))
    above = padded[:-2, 1:-1]
    below = padded[2:, 1:-1]
    left_side = padded[1:-1, :-2]
    right_side = padded[1:-1, 2:]
    total = coefs[:, :, 0][:, :, None, :] * above + coefs[:, :, 1][:, :, None, :] * below
    total = total + coefs[:, :, 2][:, :, None, :] * left_side + coefs[:, :, 3][:, :, None, :] * right_side
    return state - total


def sibling(values, level):
    order = jnp.asarray(np.arange(N_GX) ^ (1 << level), jnp.int32)
    return jnp.take(values, order, axis=1)


def reference(fields, leaf_inverse, coupling, skeleton_index, up_coef, down_coef, merge_own, merge_other, top_inverse, compress, top_couple):
    blocks = fields.reshape(N_GY, F, N_GX, NBX, Q).transpose(0, 2, 1, 3, 4)
    inverse = leaf_inverse.reshape(N_GY, N_GX, NBX, Q, Q).astype(jnp.float32)
    weights = coupling.reshape(N_GY, N_GX, NBX, K, Q).astype(jnp.float32)
    index = skeleton_index.reshape(N_GY, N_GX, NBX, K)
    own = merge_own.reshape(N_GY, N_GX, LEVELS, M, M)
    other = merge_other.reshape(N_GY, N_GX, LEVELS, M, M)
    upc = up_coef.reshape(N_GY, N_GX, LEVELS, 4, M)
    downc = down_coef.reshape(N_GY, N_GX, LEVELS, 4, M)
    topinv = top_inverse.reshape(N_GY, N_GX, M, M).astype(jnp.float32)
    comp = compress.reshape(N_GY, N_GX, KT, M).astype(jnp.float32)

    solved = jnp.einsum('yxfbq,yxbqr->yxfbr', blocks.astype(jnp.float32), inverse).astype(jnp.bfloat16)
    wide_index = jnp.broadcast_to(index[:, :, None], (N_GY, N_GX, F, NBX, K))
    picked = jnp.take_along_axis(blocks, wide_index, axis=4).astype(jnp.float32)
    state = picked - jnp.einsum('yxfbq,yxbkq->yxfbk', lax.optimization_barrier(solved).astype(jnp.float32), weights)
    state = state.reshape(N_GY, N_GX, F, M)

    for level in range(LEVELS):
        mixed = neighbour_mix(state, upc[:, :, level])
        rounded = lax.optimization_barrier(mixed.astype(jnp.bfloat16)).astype(jnp.float32)
        state = jnp.einsum('yxfm,yxmn->yxfn', rounded, own[:, :, level].astype(jnp.float32))
        state = state + jnp.einsum('yxfm,yxmn->yxfn', sibling(rounded, level), other[:, :, level].astype(jnp.float32))

    top_state = lax.optimization_barrier(state.astype(jnp.bfloat16)).astype(jnp.float32)
    small = jnp.einsum('yxfm,yxkm->yxfk', top_state, comp).astype(jnp.bfloat16)
    flat = small.transpose(2, 0, 1, 3).reshape(F, DEVICES * KT)
    coarse = jnp.dot(flat, top_couple, preferred_element_type=jnp.float32)
    coarse = coarse.reshape(F, N_GY, N_GX, KT).transpose(1, 2, 0, 3)
    coarse_round = lax.optimization_barrier(coarse.astype(jnp.bfloat16)).astype(jnp.float32)
    state = jnp.einsum('yxfm,yxmn->yxfn', top_state, topinv) + jnp.einsum('yxfk,yxkm->yxfm', coarse_round, comp)

    for level in reversed(range(LEVELS)):
        rounded = lax.optimization_barrier(state.astype(jnp.bfloat16)).astype(jnp.float32)
        local_part = jnp.einsum('yxfm,yxnm->yxfn', rounded, own[:, :, level].astype(jnp.float32))
        sent = jnp.einsum('yxfm,yxnm->yxfn', rounded, other[:, :, level].astype(jnp.float32))
        mixed = local_part + sibling(sent, level)
        state = neighbour_mix(mixed, downc[:, :, level])

    skel = state.reshape(N_GY, N_GX, F, NBX, K)
    skel_round = lax.optimization_barrier(skel.astype(jnp.bfloat16)).astype(jnp.float32)
    back = jnp.einsum('yxfbk,yxbkq->yxfbq', skel_round, weights).astype(jnp.bfloat16)
    fixed = jnp.einsum('yxfbq,yxbqr->yxfbr', lax.optimization_barrier(back).astype(jnp.float32), inverse)
    onehot = (index[..., None] == jnp.arange(Q, dtype=jnp.int32)).astype(jnp.float32)
    placed = jnp.einsum('yxfbk,yxbkq->yxfbq', skel, onehot, precision=lax.Precision.HIGHEST)
    result = solved.astype(jnp.float32) - fixed + placed
    return result.transpose(0, 2, 1, 3, 4).reshape(N_GY, F, N_GX * NBX * Q)
```

```python
import functools

import jax
import jax.numpy as jnp
from jax import lax
from jax.experimental import pallas as pl
from jax.experimental.pallas import tpu as pltpu
from jax.sharding import PartitionSpec as P

MESH = pl.DeviceIdType.MESH
BF = jnp.bfloat16
F32 = jnp.float32
SELF = 9
SELF_A = 10


def dot(a, b):
    return jnp.dot(a, b, preferred_element_type=F32)


def dot_t(a, b):
    return lax.dot_general(a, b, (((1,), (1,)), ((), ())), preferred_element_type=F32)


def up_plan(level, p, q, ny, nx):
    m = 1 << level
    s = q ^ m
    odd = (q & 1) == 1
    even = (q & 1) == 0
    sends = {
        0: (p < ny - 1, p + 1, q),
        1: (p > 0, p - 1, q),
        2: (q < nx - 1, p, q + 1),
        3: (q > 0, p, q - 1),
        4: (None, p, s),
        5: (p < ny - 1, p + 1, s),
        6: (p > 0, p - 1, s),
        7: (q < nx - 1, p, (q + 1) ^ m),
        8: (q > 0, p, (q - 1) ^ m),
    }
    takes = {
        0: p > 0,
        1: p < ny - 1,
        2: q > 0,
        3: q < nx - 1,
        4: None,
        5: p > 0,
        6: p < ny - 1,
        7: s > 0,
        8: s < nx - 1,
    }
    empty = {
        0: p == 0,
        1: p == ny - 1,
        2: q == 0,
        3: q == nx - 1,
        5: p == 0,
        6: p == ny - 1,
        7: s == 0,
        8: s == nx - 1,
    }
    where = {k: k for k in range(9)}

    def also(k, send_too, take_too):
        sends[k] = (jnp.logical_and(sends[k][0], send_too),) + sends[k][1:]
        takes[k] = jnp.logical_and(takes[k], take_too)

    if level == 0:
        also(2, odd, even)
        also(3, even, odd)
        also(7, odd, odd)
        also(8, even, even)
        where[2] = jnp.where(even, 2, 4)
        where[3] = jnp.where(even, 4, 3)
        where[7] = jnp.where(even, SELF, 7)
        where[8] = jnp.where(even, 8, SELF)
    elif level == 1:
        high = (q & m) != 0
        low = (q & m) == 0
        also(7, (((q + 1) ^ m) & m) != 0, high)
        also(8, (((q - 1) ^ m) & m) == 0, low)
        where[7] = jnp.where(low, 3, 7)
        where[8] = jnp.where(low, 8, 2)
    return sends, takes, empty, where


def down_plan(level, p, q, ny, nx):
    m = 1 << level
    s = q ^ m
    odd = (q & 1) == 1
    even = (q & 1) == 0
    sends = {
        4: (None, p, s),
        5: (p < ny - 1, p + 1, s),
        6: (p > 0, p - 1, s),
        7: (s < nx - 1, p, s + 1),
        8: (s > 0, p, s - 1),
        0: (p < ny - 1, p + 1, q),
        1: (p > 0, p - 1, q),
        2: (q < nx - 1, p, q + 1),
        3: (q > 0, p, q - 1),
    }
    takes = {
        4: None,
        0: p > 0,
        1: p < ny - 1,
        2: q > 0,
        3: q < nx - 1,
        5: p > 0,
        6: p < ny - 1,
        7: q > 0,
        8: q < nx - 1,
    }
    empty = {
        0: p == 0,
        1: p == ny - 1,
        2: q == 0,
        3: q == nx - 1,
        5: p == 0,
        6: p == ny - 1,
        7: q == 0,
        8: q == nx - 1,
    }
    where = {k: k for k in range(9)}
    if level == 0:
        sends[7] = (jnp.logical_and(sends[7][0], even),) + sends[7][1:]
        sends[8] = (jnp.logical_and(sends[8][0], odd),) + sends[8][1:]
        takes[7] = jnp.logical_and(takes[7], even)
        takes[8] = jnp.logical_and(takes[8], odd)
        where[7] = jnp.where(even, 7, SELF)
        where[8] = jnp.where(even, SELF, 8)
    return sends, takes, empty, where


def when(cond, run):
    if cond is None:
        run()
    else:
        pl.when(cond)(run)


def kernel(
    ny,
    nx,
    pack,
    fields,
    leaf_inverse,
    coupling,
    index,
    up_coef,
    down_coef,
    merge_own,
    merge_other,
    top_inverse,
    compress,
    couple,
    out,
    f_v,
    inv_v,
    coup_v,
    idx_v,
    upc_v,
    dnc_v,
    own_v,
    other_v,
    top_v,
    comp_v,
    wide_v,
    tc_v,
    sib_v,
    zbuf,
    abuf,
    c1,
    call,
    solved_v,
    d_v,
    lsem,
    up_send,
    up_recv,
    co_send,
    co_recv,
    dn_send,
    dn_recv,
    g1_send,
    g1_recv,
    g2_send,
    g2_recv,
):
    boxes, size, _ = inv_v.shape
    skel = coup_v.shape[1]
    levels = own_v.shape[0]
    kt = comp_v.shape[0]
    groups = call.shape[0]
    per_row = nx // pack
    p = lax.axis_index("gy")
    q = lax.axis_index("gx")
    me = p * nx + q
    count = ny * nx

    local = []

    def fetch(src, dst):
        copy = pltpu.make_async_copy(src, dst, lsem.at[len(local)])
        copy.start()
        local.append(copy)
        return copy

    get_f = fetch(fields.at[0], f_v)
    get_idx = fetch(index.at[0], idx_v)
    half = boxes // 2
    get_inv = [
        fetch(leaf_inverse.at[0, pl.ds(i * half, half)], inv_v.at[pl.ds(i * half, half)])
        for i in range(2)
    ]
    get_coup = fetch(coupling.at[0], coup_v)
    get_upc = fetch(up_coef.at[0], upc_v)
    get_merge = [
        (fetch(merge_own.at[0, l], own_v.at[l]), fetch(merge_other.at[0, l], other_v.at[l]))
        for l in range(levels)
    ]
    place = lax.rem(q, pack)
    wide_v[...] = jnp.zeros_like(wide_v)
    get_wide = fetch(compress.at[0], wide_v.at[pl.ds(pl.multiple_of(place * kt, kt), kt)])
    get_comp = fetch(compress.at[0], comp_v)
    get_top = fetch(top_inverse.at[0], top_v)
    get_tc = fetch(couple, tc_v)
    get_dnc = fetch(down_coef.at[0], dnc_v)

    ups = [up_plan(l, p, q, ny, nx) for l in range(levels)]
    downs = [down_plan(l, p, q, ny, nx) for l in range(levels)]

    def clear(buf, l, k):
        def run():
            buf[l, k] = jnp.zeros(buf.shape[2:], buf.dtype)

        return run

    for l in range(levels):
        for k, cond in ups[l][2].items():
            pl.when(cond)(clear(zbuf, l, k))
        for k, cond in downs[l][2].items():
            pl.when(cond)(clear(abuf, l, k))

    barrier = pltpu.get_barrier_semaphore()

    def greet(j, carry):
        t = lax.rem(me + j, count)
        pl.semaphore_signal(
            barrier, inc=1, device_id=(t // nx, lax.rem(t, nx)), device_id_type=MESH
        )
        return carry

    lax.fori_loop(1, count, greet, 0)

    get_f.wait()
    get_idx.wait()
    rows = lax.broadcasted_iota(jnp.int32, (size, skel), 0)

    def selector(k):
        return jnp.where(rows == idx_v[k : k + 1, :], 1.0, 0.0).astype(BF)

    state = []
    for k in range(boxes):
        if k % half == 0:
            get_inv[k // half].wait()
        if k == 0:
            get_coup.wait()
        b = f_v[:, k * size : (k + 1) * size]
        solved = dot(b, inv_v[k]).astype(BF)
        solved_v[:, k * size : (k + 1) * size] = solved
        state.append(dot(b, selector(k)) - dot_t(solved, coup_v[k]))
    state = jnp.concatenate(state, axis=1)

    def fold(k):
        eye = (
            lax.broadcasted_iota(jnp.int32, (skel, skel), 0)
            == lax.broadcasted_iota(jnp.int32, (skel, skel), 1)
        )
        chosen = dot_t(jnp.where(eye, 1.0, 0.0).astype(BF), selector(k))
        d_v[k] = (chosen - dot(coup_v[k], inv_v[k])).astype(BF)

    def copy_of(buf, l, source, k, target, send, recv):
        return pltpu.make_async_remote_copy(
            src_ref=buf.at[l, source],
            dst_ref=buf.at[l, k],
            send_sem=send.at[l, k],
            recv_sem=recv.at[l, k],
            device_id=target,
            device_id_type=MESH,
        )

    def start(buf, l, source, plan, k, send, recv):
        cond, tp, tq = plan[0][k]
        when(cond, lambda: copy_of(buf, l, source, k, (tp, tq), send, recv).start())

    def arrive(buf, l, source, plan, k, send, recv):
        cond = plan[1][k]
        when(cond, lambda: copy_of(buf, l, source, k, (p, q), send, recv).wait_recv())

    def sent(buf, l, source, plan, k, send, recv):
        cond = plan[0][k][0]
        when(cond, lambda: copy_of(buf, l, source, k, (p, q), send, recv).wait_send())

    def coef_copy(l):
        return pltpu.make_async_remote_copy(
            src_ref=upc_v.at[l],
            dst_ref=sib_v.at[l],
            send_sem=co_send.at[l],
            recv_sem=co_recv.at[l],
            device_id=(p, q ^ (1 << l)),
            device_id_type=MESH,
        )

    def mix(values, coefs, parts):
        total = coefs[0:1] * parts[0] + coefs[1:2] * parts[1]
        return values - (total + coefs[2:3] * parts[2] + coefs[3:4] * parts[3])

    get_upc.wait()
    pl.semaphore_wait(barrier, count - 1)
    folds = list(range(boxes))
    each = -(-boxes // levels)

    for l in range(levels):
        plan = ups[l]
        where = plan[3]
        zbuf[l, SELF] = state.astype(BF)
        if l == 0:
            coef_copy(0).start()
        for k in (4, 5, 6, 7, 8, 0, 1, 2, 3):
            start(zbuf, l, SELF, plan, k, up_send, up_recv)
        if l == 0:
            for other_level in range(1, levels):
                coef_copy(other_level).start()
        for k in folds[l * each : (l + 1) * each]:
            fold(k)
        if l > 0:
            for k in range(9):
                sent(zbuf, l - 1, SELF, ups[l - 1], k, up_send, up_recv)
        get_merge[l][0].wait()
        get_merge[l][1].wait()
        first = (0, 1, 2, 3, 4) if l == 0 else (0, 1, 2, 3)
        for k in first:
            arrive(zbuf, l, SELF, plan, k, up_send, up_recv)
        g = mix(state, upc_v[l], [zbuf[l, where[k]].astype(F32) for k in range(4)]).astype(BF)
        total = dot(g, own_v[l])
        for k in range(len(first), 9):
            arrive(zbuf, l, SELF, plan, k, up_send, up_recv)
        coef_copy(l).wait_recv()
        g = mix(
            zbuf[l, 4].astype(F32),
            sib_v[l],
            [zbuf[l, where[k]].astype(F32) for k in range(5, 9)],
        ).astype(BF)
        state = total + dot(g, other_v[l])

    top = state.astype(BF)
    get_wide.wait()
    small = dot_t(top, wide_v[...]).astype(BF)
    c1[pack - 1] = small

    def first_copy(j):
        return pltpu.make_async_remote_copy(
            src_ref=c1.at[pack - 1],
            dst_ref=c1.at[j - 1],
            send_sem=g1_send.at[j - 1],
            recv_sem=g1_recv.at[j - 1],
            device_id=(p, q ^ j),
            device_id_type=MESH,
        )

    for j in range(1, pack):
        first_copy(j).start()
    get_top.wait()
    state = dot(top, top_v[...])
    for j in range(1, pack):
        first_copy(j).wait_recv()
    joined = small.astype(F32)
    for j in range(1, pack):
        joined = joined + c1[j - 1].astype(F32)
    group = p * per_row + q // pack
    call[group] = joined.astype(BF)

    def second_copy(j):
        t = lax.rem(group + j, groups)
        return pltpu.make_async_remote_copy(
            src_ref=call.at[group],
            dst_ref=call.at[group],
            send_sem=g2_send.at[t],
            recv_sem=g2_recv.at[group],
            device_id=(t // per_row, lax.rem(t, per_row) * pack + place),
            device_id_type=MESH,
        )

    def second_from(j):
        t = lax.rem(group + j, groups)
        return pltpu.make_async_remote_copy(
            src_ref=call.at[t],
            dst_ref=call.at[t],
            send_sem=g2_send.at[t],
            recv_sem=g2_recv.at[t],
            device_id=(p, q),
            device_id_type=MESH,
        )

    def over_groups(run):
        if groups <= 8:
            for j in range(1, groups):
                run(j)
        else:
            def step(j, carry):
                run(j)
                return carry

            lax.fori_loop(1, groups, step, 0)

    over_groups(lambda j: second_copy(j).start())
    for j in range(1, pack):
        first_copy(j).wait_send()
    for k in range(9):
        sent(zbuf, levels - 1, SELF, ups[levels - 1], k, up_send, up_recv)
    for l in range(levels):
        coef_copy(l).wait_send()
    get_tc.wait()
    get_comp.wait()
    get_dnc.wait()
    over_groups(lambda j: second_from(j).wait_recv())
    if groups <= 8:
        coarse = dot_t(jnp.concatenate([call[g] for g in range(groups)], axis=1), tc_v[...])
    else:
        width = call.shape[2]

        def add(g, total):
            columns = pl.ds(pl.multiple_of(g * width, width), width)
            return total + dot_t(call[g], tc_v[:, columns])

        coarse = lax.fori_loop(0, groups, add, jnp.zeros((call.shape[1], kt), F32))
    state = state + dot(coarse.astype(BF), comp_v[...])

    for l in reversed(range(levels)):
        plan = downs[l]
        where = plan[3]
        r = state.astype(BF)
        abuf[l, SELF] = dot_t(r, other_v[l]).astype(BF)
        for k in (4, 5, 6, 7, 8):
            start(abuf, l, SELF, plan, k, dn_send, dn_recv)
        mine = dot_t(r, own_v[l])
        abuf[l, SELF_A] = mine.astype(BF)
        for k in (0, 1, 2, 3):
            start(abuf, l, SELF_A, plan, k, dn_send, dn_recv)
        if l == levels - 1:
            over_groups(lambda j: second_copy(j).wait_send())
        else:
            for k in range(9):
                source = SELF_A if k < 4 else SELF
                sent(abuf, l + 1, source, downs[l + 1], k, dn_send, dn_recv)
        for k in (4, 5, 6, 7, 8, 0, 1, 2, 3):
            arrive(abuf, l, SELF, plan, k, dn_send, dn_recv)
        parts = [
            abuf[l, where[d]].astype(F32) + abuf[l, where[5 + d]].astype(F32) for d in range(4)
        ]
        state = mix(mine + abuf[l, 4].astype(F32), dnc_v[l], parts)

    w = state.astype(BF)
    for k in range(boxes):
        part = dot(w[:, k * skel : (k + 1) * skel], d_v[k])
        columns = slice(k * size, (k + 1) * size)
        out[0, :, columns] = solved_v[:, columns].astype(F32) + part
    for k in range(9):
        source = SELF_A if k < 4 else SELF
        sent(abuf, 0, source, downs[0], k, dn_send, dn_recv)


def body(ny, nx, *args):
    (fields, leaf_inverse, coupling, index, up_coef, down_coef, merge_own, merge_other) = args[:8]
    top_inverse, compress, top_couple = args[8:]
    count = fields.shape[1]
    points = fields.shape[2]
    boxes, size = leaf_inverse.shape[1:3]
    skel = coupling.shape[2]
    levels, total = merge_own.shape[1:3]
    kt = compress.shape[1]
    pack = 128 // kt
    groups = ny * nx // pack
    couple = top_couple.T
    dma = pltpu.SemaphoreType.DMA
    scratch = [
        pltpu.VMEM((count, points), BF),
        pltpu.VMEM((boxes, size, size), BF),
        pltpu.VMEM((boxes, skel, size), BF),
        pltpu.VMEM((boxes, skel), jnp.int32),
        pltpu.VMEM((levels, 4, total), F32),
        pltpu.VMEM((levels, 4, total), F32),
        pltpu.VMEM((levels, total, total), BF),
        pltpu.VMEM((levels, total, total), BF),
        pltpu.VMEM((total, total), BF),
        pltpu.VMEM((kt, total), BF),
        pltpu.VMEM((pack * kt, total), BF),
        pltpu.VMEM(couple.shape, BF),
        pltpu.VMEM((levels, 4, total), F32),
        pltpu.VMEM((levels, 10, count, total), BF),
        pltpu.VMEM((levels, 11, count, total), BF),
        pltpu.VMEM((pack, count, pack * kt), BF),
        pltpu.VMEM((groups, count, pack * kt), BF),
        pltpu.VMEM((count, points), BF),
        pltpu.VMEM((boxes, skel, size), BF),
        dma((11 + 2 * levels,)),
        dma((levels, 9)),
        dma((levels, 9)),
        dma((levels,)),
        dma((levels,)),
        dma((levels, 9)),
        dma((levels, 9)),
        dma((pack,)),
        dma((pack,)),
        dma((groups,)),
        dma((groups,)),
    ]
    return pl.pallas_call(
        functools.partial(kernel, ny, nx, pack),
        out_shape=jax.ShapeDtypeStruct(fields.shape, F32),
        in_specs=[pl.BlockSpec(memory_space=pl.ANY)] * 11,
        out_specs=pl.BlockSpec(memory_space=pltpu.VMEM),
        scratch_shapes=scratch,
        compiler_params=pltpu.CompilerParams(
            collective_id=0, has_side_effects=True, vmem_limit_bytes=40 * 1024 * 1024
        ),
    )(
        fields, leaf_inverse, coupling, index, up_coef, down_coef, merge_own, merge_other,
        top_inverse, compress, couple,
    )


def solution(mesh):
    placed = (
        P("gy", None, "gx"),
        P("gy", "gx", None, None),
        P("gy", "gx", None, None),
        P("gy", "gx", None),
        P("gy", "gx", None, None),
        P("gy", "gx", None, None),
        P("gy", "gx", None, None),
        P("gy", "gx", None, None),
        P("gy", "gx", None),
        P("gy", "gx", None),
        P(None, ("gy", "gx")),
    )
    return jax.shard_map(
        functools.partial(body, mesh.shape["gy"], mesh.shape["gx"]),
        mesh=mesh,
        in_specs=placed,
        out_specs=P("gy", None, "gx"),
        check_vma=False,
    )
```

```python
import functools

import jax
import jax.numpy as jnp
from jax import lax
from jax.experimental import pallas as pl
from jax.experimental.pallas import tpu as pltpu
from jax.sharding import PartitionSpec as P

MESH = pl.DeviceIdType.MESH
BF = jnp.bfloat16
F32 = jnp.float32
SELF = 9
SELF_A = 10


def dot(a, b):
    return jnp.dot(a, b, preferred_element_type=F32)


def dot_t(a, b):
    return lax.dot_general(a, b, (((1,), (1,)), ((), ())), preferred_element_type=F32)


def up_plan(level, p, q, ny, nx):
    m = 1 << level
    s = q ^ m
    odd = (q & 1) == 1
    even = (q & 1) == 0
    sends = {
        0: (p < ny - 1, p + 1, q),
        1: (p > 0, p - 1, q),
        2: (q < nx - 1, p, q + 1),
        3: (q > 0, p, q - 1),
        4: (None, p, s),
        5: (p < ny - 1, p + 1, s),
        6: (p > 0, p - 1, s),
        7: (q < nx - 1, p, (q + 1) ^ m),
        8: (q > 0, p, (q - 1) ^ m),
    }
    takes = {
        0: p > 0,
        1: p < ny - 1,
        2: q > 0,
        3: q < nx - 1,
        4: None,
        5: p > 0,
        6: p < ny - 1,
        7: s > 0,
        8: s < nx - 1,
    }
    empty = {
        0: p == 0,
        1: p == ny - 1,
        2: q == 0,
        3: q == nx - 1,
        5: p == 0,
        6: p == ny - 1,
        7: s == 0,
        8: s == nx - 1,
    }
    where = {k: k for k in range(9)}

    def also(k, send_too, take_too):
        sends[k] = (jnp.logical_and(sends[k][0], send_too),) + sends[k][1:]
        takes[k] = jnp.logical_and(takes[k], take_too)

    if level == 0:
        also(2, odd, even)
        also(3, even, odd)
        also(7, odd, odd)
        also(8, even, even)
        where[2] = jnp.where(even, 2, 4)
        where[3] = jnp.where(even, 4, 3)
        where[7] = jnp.where(even, SELF, 7)
        where[8] = jnp.where(even, 8, SELF)
    elif level == 1:
        high = (q & m) != 0
        low = (q & m) == 0
        also(7, (((q + 1) ^ m) & m) != 0, high)
        also(8, (((q - 1) ^ m) & m) == 0, low)
        where[7] = jnp.where(low, 3, 7)
        where[8] = jnp.where(low, 8, 2)
    return sends, takes, empty, where


def down_plan(level, p, q, ny, nx):
    m = 1 << level
    s = q ^ m
    odd = (q & 1) == 1
    even = (q & 1) == 0
    sends = {
        4: (None, p, s),
        5: (p < ny - 1, p + 1, s),
        6: (p > 0, p - 1, s),
        7: (s < nx - 1, p, s + 1),
        8: (s > 0, p, s - 1),
        0: (p < ny - 1, p + 1, q),
        1: (p > 0, p - 1, q),
        2: (q < nx - 1, p, q + 1),
        3: (q > 0, p, q - 1),
    }
    takes = {
        4: None,
        0: p > 0,
        1: p < ny - 1,
        2: q > 0,
        3: q < nx - 1,
        5: p > 0,
        6: p < ny - 1,
        7: q > 0,
        8: q < nx - 1,
    }
    empty = {
        0: p == 0,
        1: p == ny - 1,
        2: q == 0,
        3: q == nx - 1,
        5: p == 0,
        6: p == ny - 1,
        7: q == 0,
        8: q == nx - 1,
    }
    where = {k: k for k in range(9)}
    if level == 0:
        sends[7] = (jnp.logical_and(sends[7][0], even),) + sends[7][1:]
        sends[8] = (jnp.logical_and(sends[8][0], odd),) + sends[8][1:]
        takes[7] = jnp.logical_and(takes[7], even)
        takes[8] = jnp.logical_and(takes[8], odd)
        where[7] = jnp.where(even, 7, SELF)
        where[8] = jnp.where(even, SELF, 8)
    return sends, takes, empty, where


def when(cond, run):
    if cond is None:
        run()
    else:
        pl.when(cond)(run)


def kernel(
    ny,
    nx,
    pack,
    fields,
    leaf_inverse,
    coupling,
    index,
    up_coef,
    down_coef,
    merge_own,
    merge_other,
    top_inverse,
    compress,
    couple,
    out,
    f_v,
    inv_v,
    coup_v,
    idx_v,
    upc_v,
    dnc_v,
    own_v,
    other_v,
    top_v,
    comp_v,
    wide_v,
    tc_v,
    sib_v,
    zbuf,
    abuf,
    c1,
    call,
    solved_v,
    d_v,
    lsem,
    up_send,
    up_recv,
    co_send,
    co_recv,
    dn_send,
    dn_recv,
    g1_send,
    g1_recv,
    g2_send,
    g2_recv,
):
    boxes, size, _ = inv_v.shape
    skel = coup_v.shape[1]
    levels = own_v.shape[0]
    kt = comp_v.shape[0]
    groups = call.shape[0]
    per_row = nx // pack
    p = lax.axis_index("gy")
    q = lax.axis_index("gx")
    me = p * nx + q
    count = ny * nx

    local = []

    def fetch(src, dst):
        copy = pltpu.make_async_copy(src, dst, lsem.at[len(local)])
        copy.start()
        local.append(copy)
        return copy

    get_f = fetch(fields.at[0], f_v)
    get_idx = fetch(index.at[0], idx_v)
    half = boxes // 2
    get_inv = [
        fetch(leaf_inverse.at[0, pl.ds(i * half, half)], inv_v.at[pl.ds(i * half, half)])
        for i in range(2)
    ]
    get_coup = fetch(coupling.at[0], coup_v)
    get_upc = fetch(up_coef.at[0], upc_v)
    get_merge = [
        (fetch(merge_own.at[0, l], own_v.at[l]), fetch(merge_other.at[0, l], other_v.at[l]))
        for l in range(levels)
    ]
    place = lax.rem(q, pack)
    wide_v[...] = jnp.zeros_like(wide_v)
    get_wide = fetch(compress.at[0], wide_v.at[pl.ds(pl.multiple_of(place * kt, kt), kt)])
    get_comp = fetch(compress.at[0], comp_v)
    get_top = fetch(top_inverse.at[0], top_v)
    get_tc = fetch(couple, tc_v)
    get_dnc = fetch(down_coef.at[0], dnc_v)

    ups = [up_plan(l, p, q, ny, nx) for l in range(levels)]
    downs = [down_plan(l, p, q, ny, nx) for l in range(levels)]

    def clear(buf, l, k):
        def run():
            buf[l, k] = jnp.zeros(buf.shape[2:], buf.dtype)

        return run

    for l in range(levels):
        for k, cond in ups[l][2].items():
            pl.when(cond)(clear(zbuf, l, k))
        for k, cond in downs[l][2].items():
            pl.when(cond)(clear(abuf, l, k))

    barrier = pltpu.get_barrier_semaphore()

    def greet(tp, tq):
        pl.semaphore_signal(barrier, inc=1, device_id=(tp, tq), device_id_type=MESH)

    if nx == 8 and ny == 4 and pack == 4:
        met = nx - 1
        for turn in range(1, nx):
            greet(p, q ^ turn)
        for turn in range(1, ny):
            tp = p ^ turn
            beside = jnp.logical_or(tp == p + 1, tp == p - 1)
            for flip in (0, 4):
                greet(tp, q ^ flip)

            @pl.when(beside)
            def _():
                for flip in (1, 2):
                    greet(tp, q ^ flip)

            met = met + jnp.where(beside, 4, 2)
    else:
        met = count - 1

        def greet_one(j, carry):
            t = lax.rem(me + j, count)
            greet(t // nx, lax.rem(t, nx))
            return carry

        lax.fori_loop(1, count, greet_one, 0)

    get_f.wait()
    get_idx.wait()
    rows = lax.broadcasted_iota(jnp.int32, (size, skel), 0)

    def selector(k):
        return jnp.where(rows == idx_v[k : k + 1, :], 1.0, 0.0).astype(BF)

    state = []
    for k in range(boxes):
        if k % half == 0:
            get_inv[k // half].wait()
        if k == 0:
            get_coup.wait()
        b = f_v[:, k * size : (k + 1) * size]
        solved = dot(b, inv_v[k]).astype(BF)
        solved_v[:, k * size : (k + 1) * size] = solved
        state.append(dot(b, selector(k)) - dot_t(solved, coup_v[k]))
    state = jnp.concatenate(state, axis=1)

    def fold(k):
        eye = (
            lax.broadcasted_iota(jnp.int32, (skel, skel), 0)
            == lax.broadcasted_iota(jnp.int32, (skel, skel), 1)
        )
        chosen = dot_t(jnp.where(eye, 1.0, 0.0).astype(BF), selector(k))
        d_v[k] = (chosen - dot(coup_v[k], inv_v[k])).astype(BF)

    def copy_of(buf, l, source, k, target, send, recv):
        return pltpu.make_async_remote_copy(
            src_ref=buf.at[l, source],
            dst_ref=buf.at[l, k],
            send_sem=send.at[l, k],
            recv_sem=recv.at[l, k],
            device_id=target,
            device_id_type=MESH,
        )

    def start(buf, l, source, plan, k, send, recv):
        cond, tp, tq = plan[0][k]
        when(cond, lambda: copy_of(buf, l, source, k, (tp, tq), send, recv).start())

    def arrive(buf, l, source, plan, k, send, recv):
        cond = plan[1][k]
        when(cond, lambda: copy_of(buf, l, source, k, (p, q), send, recv).wait_recv())

    def sent(buf, l, source, plan, k, send, recv):
        cond = plan[0][k][0]
        when(cond, lambda: copy_of(buf, l, source, k, (p, q), send, recv).wait_send())

    def coef_copy(l):
        return pltpu.make_async_remote_copy(
            src_ref=upc_v.at[l],
            dst_ref=sib_v.at[l],
            send_sem=co_send.at[l],
            recv_sem=co_recv.at[l],
            device_id=(p, q ^ (1 << l)),
            device_id_type=MESH,
        )

    def mix(values, coefs, parts):
        total = coefs[0:1] * parts[0] + coefs[1:2] * parts[1]
        return values - (total + coefs[2:3] * parts[2] + coefs[3:4] * parts[3])

    get_upc.wait()
    pl.semaphore_wait(barrier, met)
    folds = list(range(boxes))
    each = -(-boxes // levels)

    for l in range(levels):
        plan = ups[l]
        where = plan[3]
        zbuf[l, SELF] = state.astype(BF)
        if l == 0:
            coef_copy(0).start()
        for k in (4, 5, 6, 7, 8, 0, 1, 2, 3):
            start(zbuf, l, SELF, plan, k, up_send, up_recv)
        if l == 0:
            for other_level in range(1, levels):
                coef_copy(other_level).start()
        for k in folds[l * each : (l + 1) * each]:
            fold(k)
        if l > 0:
            for k in range(9):
                sent(zbuf, l - 1, SELF, ups[l - 1], k, up_send, up_recv)
        get_merge[l][0].wait()
        get_merge[l][1].wait()
        first = (0, 1, 2, 3, 4) if l == 0 else (0, 1, 2, 3)
        for k in first:
            arrive(zbuf, l, SELF, plan, k, up_send, up_recv)
        g = mix(state, upc_v[l], [zbuf[l, where[k]].astype(F32) for k in range(4)]).astype(BF)
        total = dot(g, own_v[l])
        for k in range(len(first), 9):
            arrive(zbuf, l, SELF, plan, k, up_send, up_recv)
        coef_copy(l).wait_recv()
        g = mix(
            zbuf[l, 4].astype(F32),
            sib_v[l],
            [zbuf[l, where[k]].astype(F32) for k in range(5, 9)],
        ).astype(BF)
        state = total + dot(g, other_v[l])

    top = state.astype(BF)
    get_wide.wait()
    small = dot_t(top, wide_v[...]).astype(BF)
    c1[pack - 1] = small

    def first_copy(j):
        return pltpu.make_async_remote_copy(
            src_ref=c1.at[pack - 1],
            dst_ref=c1.at[j - 1],
            send_sem=g1_send.at[j - 1],
            recv_sem=g1_recv.at[j - 1],
            device_id=(p, q ^ j),
            device_id_type=MESH,
        )

    for j in range(1, pack):
        first_copy(j).start()
    get_top.wait()
    state = dot(top, top_v[...])
    for j in range(1, pack):
        first_copy(j).wait_recv()
    joined = small.astype(F32)
    for j in range(1, pack):
        joined = joined + c1[j - 1].astype(F32)
    group = p * per_row + q // pack
    call[group] = joined.astype(BF)

    def second_copy(j):
        t = lax.rem(group + j, groups)
        return pltpu.make_async_remote_copy(
            src_ref=call.at[group],
            dst_ref=call.at[group],
            send_sem=g2_send.at[t],
            recv_sem=g2_recv.at[group],
            device_id=(t // per_row, lax.rem(t, per_row) * pack + place),
            device_id_type=MESH,
        )

    def second_from(j):
        t = lax.rem(group + j, groups)
        return pltpu.make_async_remote_copy(
            src_ref=call.at[t],
            dst_ref=call.at[t],
            send_sem=g2_send.at[t],
            recv_sem=g2_recv.at[t],
            device_id=(p, q),
            device_id_type=MESH,
        )

    def over_groups(run):
        if groups <= 8:
            for j in range(1, groups):
                run(j)
        else:
            def step(j, carry):
                run(j)
                return carry

            lax.fori_loop(1, groups, step, 0)

    over_groups(lambda j: second_copy(j).start())
    for j in range(1, pack):
        first_copy(j).wait_send()
    for k in range(9):
        sent(zbuf, levels - 1, SELF, ups[levels - 1], k, up_send, up_recv)
    for l in range(levels):
        coef_copy(l).wait_send()
    get_tc.wait()
    get_comp.wait()
    get_dnc.wait()
    over_groups(lambda j: second_from(j).wait_recv())
    if groups <= 8:
        coarse = dot_t(jnp.concatenate([call[g] for g in range(groups)], axis=1), tc_v[...])
    else:
        width = call.shape[2]

        def add(g, total):
            columns = pl.ds(pl.multiple_of(g * width, width), width)
            return total + dot_t(call[g], tc_v[:, columns])

        coarse = lax.fori_loop(0, groups, add, jnp.zeros((call.shape[1], kt), F32))
    state = state + dot(coarse.astype(BF), comp_v[...])

    for l in reversed(range(levels)):
        plan = downs[l]
        where = plan[3]
        r = state.astype(BF)
        abuf[l, SELF] = dot_t(r, other_v[l]).astype(BF)
        for k in (4, 5, 6, 7, 8):
            start(abuf, l, SELF, plan, k, dn_send, dn_recv)
        mine = dot_t(r, own_v[l])
        abuf[l, SELF_A] = mine.astype(BF)
        for k in (0, 1, 2, 3):
            start(abuf, l, SELF_A, plan, k, dn_send, dn_recv)
        if l == levels - 1:
            over_groups(lambda j: second_copy(j).wait_send())
        else:
            for k in range(9):
                source = SELF_A if k < 4 else SELF
                sent(abuf, l + 1, source, downs[l + 1], k, dn_send, dn_recv)
        for k in (4, 5, 6, 7, 8, 0, 1, 2, 3):
            arrive(abuf, l, SELF, plan, k, dn_send, dn_recv)
        parts = [
            abuf[l, where[d]].astype(F32) + abuf[l, where[5 + d]].astype(F32) for d in range(4)
        ]
        state = mix(mine + abuf[l, 4].astype(F32), dnc_v[l], parts)

    w = state.astype(BF)
    for k in range(boxes):
        part = dot(w[:, k * skel : (k + 1) * skel], d_v[k])
        columns = slice(k * size, (k + 1) * size)
        out[0, :, columns] = solved_v[:, columns].astype(F32) + part
    for k in range(9):
        source = SELF_A if k < 4 else SELF
        sent(abuf, 0, source, downs[0], k, dn_send, dn_recv)


def body(ny, nx, *args):
    (fields, leaf_inverse, coupling, index, up_coef, down_coef, merge_own, merge_other) = args[:8]
    top_inverse, compress, top_couple = args[8:]
    count = fields.shape[1]
    points = fields.shape[2]
    boxes, size = leaf_inverse.shape[1:3]
    skel = coupling.shape[2]
    levels, total = merge_own.shape[1:3]
    kt = compress.shape[1]
    pack = 128 // kt
    groups = ny * nx // pack
    couple = top_couple.T
    dma = pltpu.SemaphoreType.DMA
    scratch = [
        pltpu.VMEM((count, points), BF),
        pltpu.VMEM((boxes, size, size), BF),
        pltpu.VMEM((boxes, skel, size), BF),
        pltpu.VMEM((boxes, skel), jnp.int32),
        pltpu.VMEM((levels, 4, total), F32),
        pltpu.VMEM((levels, 4, total), F32),
        pltpu.VMEM((levels, total, total), BF),
        pltpu.VMEM((levels, total, total), BF),
        pltpu.VMEM((total, total), BF),
        pltpu.VMEM((kt, total), BF),
        pltpu.VMEM((pack * kt, total), BF),
        pltpu.VMEM(couple.shape, BF),
        pltpu.VMEM((levels, 4, total), F32),
        pltpu.VMEM((levels, 10, count, total), BF),
        pltpu.VMEM((levels, 11, count, total), BF),
        pltpu.VMEM((pack, count, pack * kt), BF),
        pltpu.VMEM((groups, count, pack * kt), BF),
        pltpu.VMEM((count, points), BF),
        pltpu.VMEM((boxes, skel, size), BF),
        dma((11 + 2 * levels,)),
        dma((levels, 9)),
        dma((levels, 9)),
        dma((levels,)),
        dma((levels,)),
        dma((levels, 9)),
        dma((levels, 9)),
        dma((pack,)),
        dma((pack,)),
        dma((groups,)),
        dma((groups,)),
    ]
    return pl.pallas_call(
        functools.partial(kernel, ny, nx, pack),
        out_shape=jax.ShapeDtypeStruct(fields.shape, F32),
        in_specs=[pl.BlockSpec(memory_space=pltpu.HBM)] * 11,
        out_specs=pl.BlockSpec(memory_space=pltpu.VMEM),
        scratch_shapes=scratch,
        compiler_params=pltpu.CompilerParams(
            collective_id=0, has_side_effects=True, vmem_limit_bytes=62 * 1024 * 1024
        ),
    )(
        fields, leaf_inverse, coupling, index, up_coef, down_coef, merge_own, merge_other,
        top_inverse, compress, couple,
    )


def solution(mesh):
    placed = (
        P("gy", None, "gx"),
        P("gy", "gx", None, None),
        P("gy", "gx", None, None),
        P("gy", "gx", None),
        P("gy", "gx", None, None),
        P("gy", "gx", None, None),
        P("gy", "gx", None, None),
        P("gy", "gx", None, None),
        P("gy", "gx", None),
        P("gy", "gx", None),
        P(None, ("gy", "gx")),
    )
    return jax.shard_map(
        functools.partial(body, mesh.shape["gy"], mesh.shape["gx"]),
        mesh=mesh,
        in_specs=placed,
        out_specs=P("gy", None, "gx"),
        check_vma=False,
    )
```
